32 devices in a mesh: rows: 8 (over z, x), tp: 4 (over y, core).
Axes of the slice: x: 2, y: 2, z: 4, core: 2. Of those that a mesh axis runs over, the one named last changes fastest.
Arguments:
- hidden: bfloat16 [256, 1024], P(('rows', 'tp')), may hold values from -6 to 6
- context: bfloat16 [256, 1024], P(('rows', 'tp')), may hold values from -4 to 4
- byte_input_codes: int32 [256, 4], P(('rows', 'tp')), may hold values from 0 to 255
- finish: int32 [256, 4], P('rows'), may hold values from 0 to 1, as said below
- cache_len: int32 [256], P('rows'), may hold values from 1 to 256, as said below
- embed: bfloat16 [256, 1024], replicated, may hold values from -6 to 6
- gain_local: float32 [1024], replicated, may hold values from 0.1 to 1.9
- w_in: bfloat16 [1024, 2048], replicated, may hold values from -0.1875 to 0.1875
- w_out: bfloat16 [2048, 1024], replicated, may hold values from -0.125 to 0.125
- output_norm_gain: float32 [1024], replicated, may hold values from 0.25 to 1.75
- w_vocab: bfloat16 [1024, 256], replicated, may hold values from -0.1875 to 0.1875
- w_up: bfloat16 [1024, 8192], P(None, 'rows')
- gain_global: bfloat16 [8192], P('rows'), may hold values from 0.099609375 to 1.8984375
- w_query: bfloat16 [8192, 8192], P('rows', 'tp'), may hold values from -0.0625 to 0.0625
- w_key: bfloat16 [8192, 1024], P('rows', 'tp'), may hold values from -0.0625 to 0.0625
- w_value: bfloat16 [8192, 1024], P('rows', 'tp'), may hold values from -0.0625 to 0.0625
- key_cache: bfloat16 [256, 256, 1024], P('rows', None, 'tp')
- value_cache: bfloat16 [256, 256, 1024], P('rows', None, 'tp'), may hold values from -6 to 6
- w_mix: bfloat16 [8192, 1024], P('tp'), may hold values from -0.0625 to 0.0625
Outputs:
- logits: float32 [256, 4, 256], P(('rows', 'tp'))
- context_out: bfloat16 [256, 1024], P(('rows', 'tp'))
The draws below stay inside these ranges and needn't reach their ends.
Inputs may be any that keep to these rules, and one draw needn't show every extreme that they name: Of the 8 rows of one block at one step at most 5 have finish 1; in every draw some step has 5 of them in each of the blocks that share one index of rows. `cache_len`: some row has 256.
All inputs are finite; a program needn't handle non-finite values.
Results may differ from the reference program's by a relative error of at most 0.039.
Values may be sent and summed in bfloat16 or wider, within the bound.
A program may use at most 192 MiB of HBM per device.

```python
import math
import jax
import jax.numpy as jnp
import numpy as np
from jax import lax

DL = 1024
FFL = 2048
VOC = 256
DG = 8192
HEADS = 64
KVH = 8
HD = 128
STEPS = 4
R_DEV = 8
CAP = 5
CACHE = 256
ROWS = 256
SLOTS = 160
N_ROWS = 8
N_TP = 4


def draw_finish(key, part):
    n_blocks = N_ROWS * N_TP
    key_count, key_pick, key_order = jax.random.split(key, 3)
    counts = jax.random.randint(key_count, (n_blocks, STEPS), 0, CAP + 1)
    chosen = jax.random.randint(key_pick, (2,), 0, 1 << 20)
    full_group = chosen[0] % N_ROWS
    full_step = chosen[1] % STEPS
    group_of = jnp.arange(n_blocks, dtype=jnp.int32) // N_TP
    forced = (group_of[:, None] == full_group) & (jnp.arange(STEPS, dtype=jnp.int32)[None, :] == full_step)
    counts = jnp.where(forced, CAP, counts)
    scores = jax.random.randint(key_order, (n_blocks, STEPS, R_DEV), 0, 1 << 20) * R_DEV + jnp.arange(R_DEV, dtype=jnp.int32)
    order = jnp.argsort(scores, axis=-1)
    ranks = jnp.argsort(order, axis=-1)
    marks = (ranks < counts[:, :, None]).astype(jnp.int32)
    return jnp.transpose(marks, (0, 2, 1)).reshape(n_blocks * R_DEV, STEPS)


def draw_cache_len(key, part):
    key_len, key_pick = jax.random.split(key, 2)
    lengths = jax.random.randint(key_len, (ROWS,), 1, CACHE + 1)
    target = jax.random.randint(key_pick, (), 0, ROWS)
    return jnp.where(jnp.arange(ROWS, dtype=jnp.int32) == target, CACHE, lengths).astype(jnp.int32)


def draw_w_up(key, part):
    base = jax.random.normal(key, (DL, DG), jnp.float32)
    ramp = 1.0 + 2.0 * jnp.arange(DG, dtype=jnp.float32) / (DG - 1)
    return (base * ramp[None, :] * DL ** (-0.5)).astype(jnp.bfloat16)


def draw_key_cache(key, part):
    base = jnp.clip(jax.random.normal(key, (ROWS, CACHE, KVH * HD), jnp.float32), -6.0, 6.0)
    return base.astype(jnp.bfloat16)


def set_ends(drawn, rng, low, largest):
    spot = [jax.random.randint(jax.random.fold_in(rng, axis), (), 0, length) for axis, length in enumerate(drawn.shape)]
    main_axis = drawn.shape.index(max(drawn.shape))
    next_to = spot[:main_axis] + [(spot[main_axis] + 1) % drawn.shape[main_axis]] + spot[main_axis + 1:]
    return drawn.at[tuple(spot)].set(low).at[tuple(next_to)].set(largest)


def shard_levels(own_key, extent, shards, low, top_value):
    def one(position, shards_of):
        heights = jax.random.uniform(jax.random.fold_in(jax.random.fold_in(own_key, 6), position), (shards_of,), jnp.float32, low / len(shards), top_value / len(shards))
        return jnp.repeat(jnp.exp(heights), extent[position] // shards_of).reshape((-1,) + (1,) * (len(extent) - position - 1))

    loudness = one(*shards[0])
    for cut in shards[1:]:
        loudness = loudness * one(*cut)
    return loudness


def rank_bounds(amount, lean):
    loads = [(1 << 20) // math.isqrt(grade ** lean) + 1 for grade in range(1, amount + 1)]
    scale = 1 + sum(loads) // (1 << 30)
    return np.cumsum(np.array([max(1, weight // scale) for weight in loads]))


def skewed_ids(stream_key, dims, amount, lean):
    listing = rank_bounds(amount, lean)
    pick = jax.random.randint(jax.random.fold_in(stream_key, 1), dims, 0, int(listing[amount - 1]))
    grade = jnp.searchsorted(jnp.asarray(listing, jnp.int32), pick, side="right")
    return jax.random.permutation(jax.random.fold_in(stream_key, 2), amount)[grade].astype(jnp.int32)


def noise(stream_key, extent, spread, limit, pieces=(), held_as=jnp.bfloat16):
    level = shard_levels(stream_key, extent, pieces, -0.22, 0.18) if pieces else 1.0
    values = jax.random.normal(stream_key, extent, jnp.float32) * spread * level
    return jnp.minimum(jnp.maximum(values, -limit), limit).astype(held_as)


def setup_inputs(seed: int = 0) -> dict:
    streams_of = jax.random.split(jax.random.key(seed), 20)
    hidden = noise(streams_of[0], (ROWS, DL), 1.0, 6.0, ((0, 32),))
    context = noise(streams_of[1], (ROWS, DL), 0.5, 4.0, ((0, 32),))
    byte_input_codes = set_ends(skewed_ids(streams_of[2], (ROWS, STEPS), VOC, 2), jax.random.fold_in(streams_of[2], 3), 0, VOC - 1).astype(jnp.int32)
    finish = draw_finish(jax.random.fold_in(streams_of[19], 71), 0)
    cache_len = draw_cache_len(jax.random.fold_in(streams_of[19], 71), 0)
    embed = noise(streams_of[5], (VOC, DL), 1.0, 6.0)
    gain_local = jnp.clip(1.0 + 0.18 * jax.random.normal(streams_of[6], (DL,), jnp.float32), 0.1, 1.9)
    w_in = noise(streams_of[7], (DL, FFL), DL ** -0.5, 0.1875)
    w_out = noise(streams_of[8], (FFL, DL), FFL ** -0.5, 0.125)
    output_norm_gain = jnp.clip(1.0 + 0.15 * jax.random.normal(streams_of[9], (DL,), jnp.float32), 0.25, 1.75)
    w_vocab = noise(streams_of[10], (DL, VOC), DL ** -0.5, 0.1875)
    w_up = draw_w_up(jax.random.fold_in(streams_of[19], 71), 0)
    gain_global = jnp.clip(1.0 + 0.18 * jax.random.normal(streams_of[12], (DG,), jnp.float32), 0.099609375, 1.8984375).astype(jnp.bfloat16)
    w_query = noise(streams_of[13], (DG, HEADS * HD), DG ** -0.5, 0.0625, ((0, 8), (1, 4)))
    w_key = noise(streams_of[14], (DG, KVH * HD), DG ** -0.5, 0.0625, ((0, 8), (1, 4)))
    w_value = noise(streams_of[15], (DG, KVH * HD), DG ** -0.5, 0.0625, ((0, 8), (1, 4)))
    key_cache = draw_key_cache(jax.random.fold_in(streams_of[19], 71), 0)
    value_cache = noise(streams_of[17], (ROWS, CACHE, KVH * HD), 1.0, 6.0, ((0, 8), (2, 4)))
    w_mix = noise(streams_of[18], (HEADS * HD, DL), (HEADS * HD) ** -0.5, 0.0625, ((0, 4),))
    return dict(hidden=hidden, context=context, byte_input_codes=byte_input_codes, finish=finish, cache_len=cache_len, embed=embed, gain_local=gain_local, w_in=w_in, w_out=w_out, output_norm_gain=output_norm_gain, w_vocab=w_vocab, w_up=w_up, gain_global=gain_global, w_query=w_query, w_key=w_key, w_value=w_value, key_cache=key_cache, value_cache=value_cache, w_mix=w_mix)


EPS = 1e-05

def rms_scale(values, gain):
    mean_sq = lax.optimization_barrier(jnp.mean(values * values, axis=-1, keepdims=True))
    return values * lax.rsqrt(mean_sq + EPS) * gain

def slot_picker(finished, capacity):
    ranked = jnp.cumsum(finished, axis=-1) - 1
    slot_ids = jnp.arange(capacity, dtype=jnp.int32)
    chosen = (finished[..., None, :] == 1) & (ranked[..., None, :] == slot_ids[:, None])
    return chosen.astype(jnp.int32)

def attend(query_rows, fresh_key_rows, new_values, keys, values, lengths):
    head_size = query_rows.shape[-1]
    logit_scale = 1.0 / jnp.sqrt(jnp.float32(head_size))
    query_rows = query_rows.astype(jnp.float32)
    scores = jnp.einsum('bkgd,btkd->bkgt', query_rows, keys.astype(jnp.float32)) * logit_scale
    positions = jnp.arange(keys.shape[1], dtype=jnp.int32)
    valid = positions[None, :] < lengths[:, None]
    scores = jnp.where(valid[:, None, None, :], scores, -jnp.inf)
    self_token = jnp.einsum('orey,ory->ore', query_rows, fresh_key_rows.astype(jnp.float32)) * logit_scale
    top = jnp.maximum(lax.optimization_barrier(jnp.max(scores, axis=-1)), self_token)
    weights = jnp.exp(scores - top[..., None])
    own_weight = jnp.exp(self_token - top)
    total = lax.optimization_barrier(jnp.sum(weights, axis=-1)) + own_weight
    probs = (weights / total[..., None]).astype(jnp.bfloat16)
    own_prob = (own_weight / total).astype(jnp.bfloat16)
    mixed = jnp.einsum('bkgt,btkd->bkgd', probs.astype(jnp.float32), values.astype(jnp.float32))
    mixed = mixed + own_prob.astype(jnp.float32)[..., None] * new_values.astype(jnp.float32)[:, :, None, :]
    return mixed.astype(jnp.bfloat16).reshape(query_rows.shape[0], -1)

def reference(hidden, context, byte_input_codes, finish, cache_len, embed, gain_local, w_in, w_out, output_norm_gain, w_vocab, w_up, gain_global, w_query, w_key, w_value, key_cache, value_cache, w_mix):
    n_blocks = N_ROWS * N_TP
    group = HEADS // KVH
    state = hidden.astype(jnp.float32)
    ctx = context
    logit_list = []
    for byte_step in range(STEPS):
        x_val = state + embed[byte_input_codes[:, byte_step]].astype(jnp.float32) + ctx.astype(jnp.float32)
        normed_loc = rms_scale(x_val, gain_local).astype(jnp.bfloat16)
        inner = jax.nn.silu(jnp.dot(normed_loc, w_in, preferred_element_type=jnp.float32)).astype(jnp.bfloat16)
        state = x_val + jnp.dot(inner, w_out, preferred_element_type=jnp.float32)
        final = rms_scale(state, output_norm_gain).astype(jnp.bfloat16)
        logit_list.append(jnp.dot(final, w_vocab, preferred_element_type=jnp.float32))
        finished = finish[:, byte_step].reshape(n_blocks, R_DEV)
        picker = slot_picker(finished, CAP)
        local_row = lax.optimization_barrier(jnp.sum(picker * jnp.arange(R_DEV, dtype=jnp.int32), axis=-1))
        row_index = (local_row + jnp.arange(n_blocks, dtype=jnp.int32)[:, None] * R_DEV).reshape(SLOTS).astype(jnp.int32)
        state_rows = state.astype(jnp.bfloat16).astype(jnp.float32).reshape(n_blocks, R_DEV, DL)
        slot_h = jnp.einsum('dcr,drk->dck', picker.astype(jnp.float32), state_rows).astype(jnp.bfloat16).reshape(SLOTS, DL)
        upper = jnp.dot(slot_h, w_up, preferred_element_type=jnp.float32)
        inv = lax.rsqrt(lax.optimization_barrier(jnp.sum(upper * upper, axis=1)) / DG + EPS)[:, None]
        normed = (upper * gain_global.astype(jnp.float32)).astype(jnp.bfloat16)
        query = (jnp.dot(normed, w_query, preferred_element_type=jnp.float32) * inv).astype(jnp.bfloat16)
        new_key = (jnp.dot(normed, w_key, preferred_element_type=jnp.float32) * inv).astype(jnp.bfloat16)
        new_value = (jnp.dot(normed, w_value, preferred_element_type=jnp.float32) * inv).astype(jnp.bfloat16)
        keys = key_cache[row_index].reshape(SLOTS, CACHE, KVH, HD)
        values = value_cache[row_index].reshape(SLOTS, CACHE, KVH, HD)
        lengths = cache_len[row_index]
        attended = attend(query.reshape(SLOTS, KVH, group, HD), new_key.reshape(SLOTS, KVH, HD), new_value.reshape(SLOTS, KVH, HD), keys, values, lengths)
        patch_context_state = jnp.dot(attended, w_mix, preferred_element_type=jnp.float32).astype(jnp.bfloat16)
        delivered = jnp.einsum('dcr,dck->drk', picker.astype(jnp.float32), patch_context_state.astype(jnp.float32).reshape(n_blocks, CAP, DL))
        delivered = delivered.reshape(ROWS, DL).astype(jnp.bfloat16)
        ctx = jnp.where((finish[:, byte_step] == 1)[:, None], delivered, ctx)
    return (jnp.stack(logit_list, axis=1), ctx)
```

```python
import functools

import jax
import jax.numpy as jnp
import numpy as np
from jax import lax
from jax.experimental import pallas as pl
from jax.experimental.pallas import tpu as pltpu
from jax.sharding import PartitionSpec as P

HD = 128
CAP = 5
R_DEV = 8
EPS = 1e-05
MESH = pl.DeviceIdType.MESH
F32 = jnp.float32
BF16 = jnp.bfloat16


def rms_scale(values, gain):
    mean_sq = jnp.mean(values * values, axis=-1, keepdims=True)
    return values * lax.rsqrt(mean_sq + EPS) * gain


def slot_picker(finished):
    ranked = jnp.cumsum(finished, axis=-1) - 1
    slot_ids = jnp.arange(CAP, dtype=jnp.int32)
    chosen = (finished[..., None, :] == 1) & (ranked[..., None, :] == slot_ids[:, None])
    return chosen.astype(jnp.int32)


def unpack_matrix():
    m = np.zeros((384, 256), np.float32)
    for d in range(16):
        for k in range(4):
            for c in range(4):
                m[k * 64 + d * 4 + c, d * 16 + 4 * k + c] = 1
        for k in range(8):
            m[256 + k * 16 + d, d * 16 + k] = 1
    return m


def dot(a, b):
    return jnp.dot(a, b, preferred_element_type=F32)


def kernel(
    n_rows, n_tp, n_steps,
    idx_ref, len_ref, hidden_ref, context_ref, oh_ref, pick_ref, pickt_ref, unpack_ref,
    gl_ref, og_ref, gg_ref,
    embed_hbm, w_in_hbm, w_out_hbm, w_vocab_hbm, w_up_hbm, w_q_hbm, w_k_hbm, w_v_hbm,
    kc_hbm, vc_hbm, w_mix_hbm,
    logits_ref, ctx_out_ref,
    embed, w_in, w_out, w_vocab, w_up, w_q, w_k, w_v, kc, vc, w_mix,
    emb_s, state_s, ctx_s, packm, packt, ag_send, ag_recv, h_s,
    qs_main, tail_f, qs_tail, qr_main, qr_tail, ss_send, ss_recv,
    qf, tsum, scores, selfs, probs, owns, of, mix_s, tp_recv,
    load_sem, ag_ssem, ag_rsem, q_ssem, q_rsem, tp_ssem, tp_rsem,
):
    r = lax.axis_index("rows")
    t = lax.axis_index("tp")
    n_dev = n_rows * n_tp
    me = r * n_tp + t
    dl = hidden_ref.shape[1]
    q_cols, kv_cols = w_q.shape[1], w_k.shape[1]
    cols = q_cols + 2 * kv_cols
    kv_local = kv_cols // HD
    n_heads = q_cols // HD
    group = n_heads // kv_local
    n_main, n_tail = 4 * n_dev, n_dev
    g_main, g_tail = 4 * n_tp, n_tp
    chunks = 16 // n_tp
    cw = cols // chunks
    hs = -(-(CAP * n_tp) // 8) * 8
    vocab = w_vocab.shape[1]
    dg = n_rows * w_up.shape[1]
    scale = 1.0 / np.float32(np.sqrt(np.float32(HD)))

    loads = [
        pltpu.make_async_copy(a, b, load_sem.at[i])
        for i, (a, b) in enumerate(
            [
                (embed_hbm, embed), (w_in_hbm, w_in), (w_out_hbm, w_out),
                (w_vocab_hbm, w_vocab), (w_up_hbm, w_up), (w_q_hbm, w_q),
                (w_k_hbm, w_k), (w_v_hbm, w_v), (kc_hbm, kc), (vc_hbm, vc),
                (w_mix_hbm, w_mix),
            ]
        )
    ]
    for c in loads:
        c.start()

    barrier = pltpu.get_barrier_semaphore()

    def greet(i, carry):
        to = lax.rem(me + i, n_dev)
        pl.semaphore_signal(
            barrier, inc=1, device_id=(to // n_tp, lax.rem(to, n_tp)), device_id_type=MESH
        )
        return carry

    lax.fori_loop(1, n_dev, greet, 0)

    state_s[...] = hidden_ref[...].astype(F32)
    ctx_s[...] = context_ref[...].astype(F32)
    ss_send[...] = jnp.zeros_like(ss_send)
    of[...] = jnp.zeros_like(of)
    packt[...] = jnp.zeros_like(packt)
    loads[0].wait()
    emb_s[...] = dot(oh_ref[...], embed[...])
    pl.semaphore_wait(barrier, n_dev - 1)

    def ag_copy(s, to, src):
        return pltpu.make_async_remote_copy(
            src_ref=ag_send,
            dst_ref=ag_recv.at[s, pl.ds(pl.multiple_of(src * 16, 16), 16)],
            send_sem=ag_ssem.at[to],
            recv_sem=ag_rsem.at[s, src],
            device_id=(to // n_tp, lax.rem(to, n_tp)),
            device_id_type=MESH,
        )

    def q_copies(s, to, src):
        return [
            pltpu.make_async_remote_copy(
                src_ref=a.at[pl.ds(pl.multiple_of(to * rows, rows), rows)],
                dst_ref=b.at[s, pl.ds(pl.multiple_of(src * rows, rows), rows)],
                send_sem=q_ssem.at[i, to],
                recv_sem=q_rsem.at[s, i, src],
                device_id=(to, t),
                device_id_type=MESH,
            )
            for i, (a, b, rows) in enumerate(
                [(qs_main, qr_main, g_main), (qs_tail, qr_tail, 16), (ss_send, ss_recv, hs)]
            )
        ]

    def tp_copy(s, to, src):
        return pltpu.make_async_remote_copy(
            src_ref=mix_s.at[pl.ds(pl.multiple_of(to * 8, 8), 8)],
            dst_ref=tp_recv.at[s, pl.ds(pl.multiple_of(src * 8, 8), 8)],
            send_sem=tp_ssem.at[to],
            recv_sem=tp_rsem.at[s, src],
            device_id=(r, to),
            device_id_type=MESH,
        )

    def step(s, carry):
        s8 = pl.multiple_of(s * 8, 8)
        x = state_s[...] + emb_s[pl.ds(s8, 8), :] + ctx_s[...]
        a = rms_scale(x, gl_ref[...]).astype(BF16)

        @pl.when(s == 0)
        def _():
            loads[1].wait()
            loads[2].wait()

        f = dot(a, w_in[...])
        f = (f / (1.0 + jnp.exp(-f))).astype(BF16)
        state = x + dot(f, w_out[...])
        state_s[...] = state
        slots = dot(pick_ref[s].astype(BF16), state.astype(BF16))
        for k in range(4):
            w = dl // 4
            packm[4 * k : 4 * k + 4, :] = slots[0:4, w * k : w * k + w]
        for k in range(8):
            w = dl // 8
            packt[k : k + 1, :] = slots[4:5, w * k : w * k + w]
        packed = jnp.concatenate([packm[...], packt[...]], axis=1).astype(BF16)
        ag_send[...] = packed

        def send(i, c):
            ag_copy(s, lax.rem(me + i, n_dev), me).start()
            return c

        lax.fori_loop(1, n_dev, send, 0)
        ag_recv[s, pl.ds(pl.multiple_of(me * 16, 16), 16), :] = packed

        @pl.when(s == 0)
        def _():
            loads[3].wait()
            loads[4].wait()

        final = rms_scale(state, og_ref[...]).astype(BF16)
        logits_ref[:, pl.ds(pl.multiple_of(s * vocab, vocab), vocab)] = dot(final, w_vocab[...])

        def recv(i, c):
            src = lax.rem(me + n_dev - i, n_dev)
            ag_copy(s, me, src).wait_recv()
            return c

        lax.fori_loop(1, n_dev, recv, 0)

        for g in range(n_dev // 16):
            got = ag_recv[s, g * 256 : g * 256 + 256, :]
            m = dot(unpack_ref[0:256, :], got[:, 0:256]).astype(BF16)
            tl = dot(unpack_ref[256:384, :], got[:, 256:384]).astype(BF16)
            for k in range(4):
                h_s[g * 64 : g * 64 + 64, 256 * k : 256 * k + 256] = m[k * 64 : k * 64 + 64]
            for k in range(8):
                h_s[n_main + g * 16 : n_main + g * 16 + 16, 128 * k : 128 * k + 128] = tl[
                    k * 16 : k * 16 + 16
                ]
        up = dot(h_s[...], w_up[...])
        ss = jnp.broadcast_to(jnp.sum(up * up, axis=1, keepdims=True), (up.shape[0], 128))
        for g in range(n_rows):
            ss_send[g * hs : g * hs + g_main, :] = ss[g * g_main : (g + 1) * g_main]
            ss_send[g * hs + g_main : g * hs + g_main + g_tail, :] = ss[
                n_main + g * g_tail : n_main + (g + 1) * g_tail
            ]
        normed = (up * gg_ref[...].astype(F32)).astype(BF16)

        @pl.when(s == 0)
        def _():
            loads[5].wait()
            loads[6].wait()
            loads[7].wait()

        q = dot(normed, w_q[...])
        kv = jnp.concatenate([dot(normed, w_k[...]), dot(normed, w_v[...])], axis=1)
        qs_main[:, 0:q_cols] = q[0:n_main].astype(BF16)
        qs_main[:, q_cols:cols] = kv[0:n_main].astype(BF16)
        tail = jnp.concatenate([q[n_main:], kv[n_main:]], axis=1)
        for g in range(n_rows):
            for k in range(chunks):
                at = g * 16 + k * n_tp
                tail_f[at : at + n_tp, :] = tail[g * n_tp : (g + 1) * n_tp, cw * k : cw * k + cw]
        qs_tail[...] = tail_f[...].astype(BF16)

        def qsend(i, c):
            for copy in q_copies(s, lax.rem(r + i, n_rows), r):
                copy.start()
            return c

        lax.fori_loop(1, n_rows, qsend, 0)
        for a_ref, b_ref, rows in (
            (qs_main, qr_main, g_main), (qs_tail, qr_tail, 16), (ss_send, ss_recv, hs)
        ):
            at = pl.ds(pl.multiple_of(r * rows, rows), rows)
            b_ref[s, at, :] = a_ref[at, :]

        def qrecv(i, c):
            for copy in q_copies(s, r, lax.rem(r + n_rows - i, n_rows)):
                copy.wait_recv()
            return c

        lax.fori_loop(1, n_rows, qrecv, 0)

        inv = ss_recv[s, 0:hs, :]
        tsum_v = qr_tail[s, 0:16, :].astype(F32)
        for g in range(1, n_rows):
            inv = inv + ss_recv[s, g * hs : (g + 1) * hs, :]
            tsum_v = tsum_v + qr_tail[s, g * 16 : (g + 1) * 16, :].astype(F32)
        inv = lax.rsqrt(inv * (1.0 / dg) + EPS)
        tsum[...] = tsum_v
        for h in range(cols // HD):
            at = slice(h * HD, (h + 1) * HD)
            v = qr_main[s, 0:g_main, at].astype(F32)
            for g in range(1, n_rows):
                v = v + qr_main[s, g * g_main : (g + 1) * g_main, at].astype(F32)
            qf[h * hs : h * hs + g_main, :] = (v * inv[0:g_main]).astype(BF16).astype(F32)
            k, off = (h * HD) // cw, (h * HD) % cw
            tv = tsum[k * n_tp : (k + 1) * n_tp, off : off + HD]
            qf[h * hs + g_main : h * hs + g_main + g_tail, :] = (
                (tv * inv[g_main : g_main + g_tail]).astype(BF16).astype(F32)
            )

        @pl.when(s == 0)
        def _():
            loads[8].wait()
            loads[9].wait()
            loads[10].wait()

        positions = lax.broadcasted_iota(jnp.int32, (group, kc.shape[1]), 1)
        n_slots = n_tp * CAP
        pairs = []
        for tt in range(n_tp):
            for c in range(CAP):
                j = tt * 4 + c if c < 4 else g_main + tt
                for v in range(kv_local):
                    pairs.append((tt, c, j, v))
        for p, (tt, c, j, v) in enumerate(pairs):
            row = idx_ref[s * n_slots + tt * CAP + c]
            length = len_ref[s * n_slots + tt * CAP + c]
            q8 = qf[pl.ds(v * group * hs + j, group, stride=hs), :]
            nk = qf[pl.ds((n_heads + v) * hs + j, 1), :]
            keys = kc[row, :, v * HD : (v + 1) * HD]
            sc = lax.dot_general(
                q8.astype(BF16), keys, (((1,), (1,)), ((), ())), preferred_element_type=F32
            )
            scores[p * group : (p + 1) * group, :] = jnp.where(
                positions < length, sc * scale, -jnp.inf
            )
            selfs[p * group : (p + 1) * group, :] = jnp.broadcast_to(
                jnp.sum(q8 * nk, axis=1, keepdims=True) * scale, (group, 128)
            )
        sc = scores[...]
        own = selfs[:, 0:1]
        top = jnp.maximum(jnp.max(sc, axis=1, keepdims=True), own)
        w = jnp.exp(sc - top)
        wo = jnp.exp(own - top)
        inv_total = 1.0 / (jnp.sum(w, axis=1, keepdims=True) + wo)
        probs[...] = (w * inv_total).astype(BF16).astype(F32)
        owns[...] = jnp.broadcast_to((wo * inv_total).astype(BF16).astype(F32), owns.shape)
        os = n_tp * 8
        for p, (tt, c, j, v) in enumerate(pairs):
            row = idx_ref[s * n_slots + tt * CAP + c]
            nv = qf[pl.ds((n_heads + kv_local + v) * hs + j, 1), :]
            values = vc[row, :, v * HD : (v + 1) * HD]
            pr = probs[p * group : (p + 1) * group, :].astype(BF16)
            o = dot(pr, values) + owns[p * group : (p + 1) * group, :] * nv
            of[pl.ds(v * group * os + tt * 8 + c, group, stride=os), :] = o

        att = jnp.concatenate(
            [of[h * os : (h + 1) * os, :].astype(BF16) for h in range(n_heads)], axis=1
        )
        mix_s[...] = dot(att, w_mix[...])

        def tsend(i, c):
            tp_copy(s, lax.rem(t + i, n_tp), t).start()
            return c

        lax.fori_loop(1, n_tp, tsend, 0)
        at = pl.ds(pl.multiple_of(t * 8, 8), 8)
        tp_recv[s, at, :] = mix_s[at, :]

        def trecv(i, c):
            tp_copy(s, t, lax.rem(t + n_tp - i, n_tp)).wait_recv()
            return c

        lax.fori_loop(1, n_tp, trecv, 0)
        patch = tp_recv[s, 0:8, :]
        for g in range(1, n_tp):
            patch = patch + tp_recv[s, g * 8 : (g + 1) * 8, :]
        back = pickt_ref[s]
        delivered = dot(back.astype(BF16), patch.astype(BF16))
        done = jnp.sum(back, axis=1, keepdims=True) > 0.0
        ctx_s[...] = jnp.where(done, delivered, ctx_s[...])

        def drain_ag(i, c):
            ag_copy(s, lax.rem(me + i, n_dev), me).wait_send()
            return c

        def drain_q(i, c):
            for copy in q_copies(s, lax.rem(r + i, n_rows), r):
                copy.wait_send()
            return c

        def drain_tp(i, c):
            tp_copy(s, lax.rem(t + i, n_tp), t).wait_send()
            return c

        lax.fori_loop(1, n_dev, drain_ag, 0)
        lax.fori_loop(1, n_rows, drain_q, 0)
        lax.fori_loop(1, n_tp, drain_tp, 0)
        return carry

    lax.fori_loop(0, n_steps, step, 0)
    ctx_out_ref[...] = ctx_s[...].astype(BF16)


def on_device(
    hidden, context, byte_input_codes, finish, cache_len, embed, gain_local, w_in, w_out,
    output_norm_gain, w_vocab, w_up, gain_global, w_query, w_key, w_value, key_cache,
    value_cache, w_mix,
):
    n_rows, n_tp = lax.axis_size("rows"), lax.axis_size("tp")
    t = lax.axis_index("tp")
    rows, dl = hidden.shape
    n_steps = byte_input_codes.shape[1]
    vocab = embed.shape[0]
    n_dev = n_rows * n_tp
    slots = n_tp * CAP
    q_cols, kv_cols = w_query.shape[1], w_key.shape[1]
    cols = q_cols + 2 * kv_cols
    hs = -(-slots // 8) * 8
    cache = key_cache.shape[1]
    n_heads = q_cols // HD
    att_rows = slots * n_heads
    cw = cols * n_tp // 16

    oh = (
        byte_input_codes.T.reshape(n_steps * rows, 1) == jnp.arange(vocab, dtype=jnp.int32)[None, :]
    ).astype(BF16)
    picker = slot_picker(finish.T.reshape(n_steps, n_tp, rows))
    local = jnp.sum(picker * jnp.arange(rows, dtype=jnp.int32), axis=-1)
    row_index = (local + jnp.arange(n_tp, dtype=jnp.int32)[:, None] * rows).reshape(-1)
    lengths = jnp.take(cache_len, row_index, axis=0)
    mine = lax.dynamic_index_in_dim(picker, t, 1, keepdims=False).astype(F32)
    pick = jnp.pad(mine, ((0, 0), (0, 8 - CAP), (0, 0)))
    pickt = pick.transpose(0, 2, 1)

    vm = pl.BlockSpec(memory_space=pltpu.VMEM)
    sm = pl.BlockSpec(memory_space=pltpu.SMEM)
    anys = pl.BlockSpec(memory_space=pl.ANY)
    weights = (
        embed, w_in, w_out, w_vocab, w_up, w_query, w_key, w_value, key_cache, value_cache, w_mix
    )
    dma = pltpu.SemaphoreType.DMA
    logits, ctx = pl.pallas_call(
        functools.partial(kernel, n_rows, n_tp, n_steps),
        out_shape=(
            jax.ShapeDtypeStruct((rows, n_steps * vocab), F32),
            jax.ShapeDtypeStruct((rows, dl), BF16),
        ),
        in_specs=[sm, sm] + [vm] * 9 + [anys] * len(weights),
        out_specs=(vm, vm),
        scratch_shapes=[pltpu.VMEM(w.shape, w.dtype) for w in weights]
        + [
            pltpu.VMEM((n_steps * rows, dl), F32),
            pltpu.VMEM((rows, dl), F32),
            pltpu.VMEM((rows, dl), F32),
            pltpu.VMEM((16, dl // 4), F32),
            pltpu.VMEM((16, dl // 8), F32),
            pltpu.VMEM((16, 3 * dl // 8), BF16),
            pltpu.VMEM((n_steps, n_dev * 16, 3 * dl // 8), BF16),
            pltpu.VMEM((5 * n_dev, dl), BF16),
            pltpu.VMEM((4 * n_dev, cols), BF16),
            pltpu.VMEM((16 * n_rows, cw), F32),
            pltpu.VMEM((16 * n_rows, cw), BF16),
            pltpu.VMEM((n_steps, 4 * n_dev, cols), BF16),
            pltpu.VMEM((n_steps, 16 * n_rows, cw), BF16),
            pltpu.VMEM((n_rows * hs, 128), F32),
            pltpu.VMEM((n_steps, n_rows * hs, 128), F32),
            pltpu.VMEM((cols // HD * hs, HD), F32),
            pltpu.VMEM((16, cw), F32),
            pltpu.VMEM((att_rows, cache), F32),
            pltpu.VMEM((att_rows, 128), F32),
            pltpu.VMEM((att_rows, cache), F32),
            pltpu.VMEM((att_rows, 128), F32),
            pltpu.VMEM((n_heads * n_tp * 8, HD), F32),
            pltpu.VMEM((n_tp * 8, dl), F32),
            pltpu.VMEM((n_steps, n_tp * 8, dl), F32),
            dma((len(weights),)),
            dma((n_dev,)),
            dma((n_steps, n_dev)),
            dma((3, n_rows)),
            dma((n_steps, 3, n_rows)),
            dma((n_tp,)),
            dma((n_steps, n_tp)),
        ],
        compiler_params=pltpu.CompilerParams(
            collective_id=0, has_side_effects=True, vmem_limit_bytes=56 * 1024 * 1024
        ),
    )(
        row_index, lengths, hidden, context, oh, pick, pickt,
        jnp.asarray(unpack_matrix(), BF16),
        gain_local.reshape(1, -1), output_norm_gain.reshape(1, -1), gain_global.reshape(1, -1),
        *weights,
    )
    return logits.reshape(rows, n_steps, vocab), ctx


def solution(mesh):
    in_specs = (
        P(("rows", "tp"), None),
        P(("rows", "tp"), None),
        P(("rows", "tp"), None),
        P("rows", None),
        P("rows"),
        P(),
        P(),
        P(),
        P(),
        P(),
        P(),
        P(None, "rows"),
        P("rows"),
        P("rows", "tp"),
        P("rows", "tp"),
        P("rows", "tp"),
        P("rows", None, "tp"),
        P("rows", None, "tp"),
        P("tp", None),
    )
    out_specs = (P(("rows", "tp"), None, None), P(("rows", "tp"), None))
    return jax.shard_map(
        on_device, mesh=mesh, in_specs=in_specs, out_specs=out_specs, check_vma=False
    )
```

```python
import functools

import jax
import jax.numpy as jnp
import numpy as np
from jax import lax
from jax.experimental import pallas as pl
from jax.experimental.pallas import tpu as pltpu
from jax.sharding import PartitionSpec as P

HD = 128
CAP = 5
R_DEV = 8
EPS = 1e-05
MESH = pl.DeviceIdType.MESH
F32 = jnp.float32
BF16 = jnp.bfloat16


def rms_scale(values, gain):
    mean_sq = jnp.mean(values * values, axis=-1, keepdims=True)
    return values * lax.rsqrt(mean_sq + EPS) * gain


def slot_picker(finished):
    ranked = jnp.cumsum(finished, axis=-1) - 1
    slot_ids = jnp.arange(CAP, dtype=jnp.int32)
    chosen = (finished[..., None, :] == 1) & (ranked[..., None, :] == slot_ids[:, None])
    return chosen.astype(jnp.int32)


def unpack_matrix():
    m = np.zeros((384, 256), np.float32)
    for d in range(16):
        for k in range(4):
            for c in range(4):
                m[k * 64 + d * 4 + c, d * 16 + 4 * k + c] = 1
        for k in range(8):
            m[256 + k * 16 + d, d * 16 + k] = 1
    return m


def dot(a, b):
    return jnp.dot(a, b, preferred_element_type=F32)


def kernel(
    n_rows, n_tp, n_steps,
    idx_ref, len_ref, hidden_ref, context_ref, oh_ref, pick_ref, pickt_ref, unpack_ref,
    gl_ref, og_ref, gg_ref,
    embed_hbm, w_in_hbm, w_out_hbm, w_vocab_hbm, w_up_hbm, w_q_hbm, w_k_hbm, w_v_hbm,
    kc_hbm, vc_hbm, w_mix_hbm,
    logits_ref, ctx_out_ref,
    embed, w_in, w_out, w_vocab, w_up, w_q, w_k, w_v, kc, vc, w_mix,
    emb_s, state_s, ctx_s, packm, packt, ag_send, ag_recv, h_s,
    qs_main, tail_f, qs_tail, xr_main, xr_tail, ys_main, ys_tail, qr_main, qr_tail, ss_send, ss_recv,
    qf, tsum, scores, selfs, probs, owns, of, mix_s, tp_recv,
    load_sem, ag_ssem, fw_ssem, ag_rsem, x_ssem, x_rsem, z_ssem, z_rsem, n_ssem, n_rsem,
    tp_ssem, tp_rsem,
):
    r = lax.axis_index("rows")
    t = lax.axis_index("tp")
    n_dev = n_rows * n_tp
    me = r * n_tp + t
    dl = hidden_ref.shape[1]
    q_cols, kv_cols = w_q.shape[1], w_k.shape[1]
    cols = q_cols + 2 * kv_cols
    kv_local = kv_cols // HD
    n_heads = q_cols // HD
    group = n_heads // kv_local
    n_main, n_tail = 4 * n_dev, n_dev
    g_main, g_tail = 4 * n_tp, n_tp
    chunks = 16 // n_tp
    cw = cols // chunks
    hs = -(-(CAP * n_tp) // 8) * 8
    outer = min(4, n_rows)
    inner = n_rows // outer
    hi, lo = r // inner, lax.rem(r, inner)
    vocab = w_vocab.shape[1]
    dg = n_rows * w_up.shape[1]
    scale = 1.0 / np.float32(np.sqrt(np.float32(HD)))

    loads = [
        pltpu.make_async_copy(a, b, load_sem.at[i])
        for i, (a, b) in enumerate(
            [
                (embed_hbm, embed), (w_in_hbm, w_in), (w_out_hbm, w_out),
                (w_vocab_hbm, w_vocab), (w_up_hbm, w_up), (w_q_hbm, w_q),
                (w_k_hbm, w_k), (w_v_hbm, w_v), (kc_hbm, kc), (vc_hbm, vc),
                (w_mix_hbm, w_mix),
            ]
        )
    ]
    for c in loads:
        c.start()

    barrier = pltpu.get_barrier_semaphore()

    def greet(i, carry):
        to = lax.rem(me + i, n_dev)
        pl.semaphore_signal(
            barrier, inc=1, device_id=(to // n_tp, lax.rem(to, n_tp)), device_id_type=MESH
        )
        return carry

    lax.fori_loop(1, n_dev, greet, 0)

    state_s[...] = hidden_ref[...].astype(F32)
    ctx_s[...] = context_ref[...].astype(F32)
    ss_send[...] = jnp.zeros_like(ss_send)
    of[...] = jnp.zeros_like(of)
    packt[...] = jnp.zeros_like(packt)
    loads[0].wait()
    emb_s[...] = dot(oh_ref[...], embed[...])
    pl.semaphore_wait(barrier, n_dev - 1)

    def ag_rows(s, to, src):
        slot = src * n_tp + t
        return pltpu.make_async_remote_copy(
            src_ref=ag_send,
            dst_ref=ag_recv.at[s, pl.ds(pl.multiple_of(slot * 16, 16), 16)],
            send_sem=ag_ssem.at[to],
            recv_sem=ag_rsem.at[s, slot],
            device_id=(to, t),
            device_id_type=MESH,
        )

    def ag_own(s, to, src):
        slot = r * n_tp + src
        return pltpu.make_async_remote_copy(
            src_ref=ag_send,
            dst_ref=ag_recv.at[s, pl.ds(pl.multiple_of(slot * 16, 16), 16)],
            send_sem=fw_ssem.at[r, to],
            recv_sem=ag_rsem.at[s, slot],
            device_id=(r, to),
            device_id_type=MESH,
        )

    def ag_forward(s, row, to, src):
        slot = row * n_tp + src
        at = pl.ds(pl.multiple_of(slot * 16, 16), 16)
        return pltpu.make_async_remote_copy(
            src_ref=ag_recv.at[s, at],
            dst_ref=ag_recv.at[s, at],
            send_sem=fw_ssem.at[row, to],
            recv_sem=ag_rsem.at[s, slot],
            device_id=(r, to),
            device_id_type=MESH,
        )

    def x_copy(s, p, to, src):
        if p < chunks:
            a, b, rows = qs_main.at[p], xr_main.at[s, p], outer * g_main
        else:
            a, b, rows = qs_tail, xr_tail.at[s], outer * 16
        return pltpu.make_async_remote_copy(
            src_ref=a.at[pl.ds(pl.multiple_of(to * rows, 16), rows)],
            dst_ref=b.at[src],
            send_sem=x_ssem.at[p, to],
            recv_sem=x_rsem.at[s, p, src],
            device_id=(hi * inner + to, t),
            device_id_type=MESH,
        )

    def z_copy(s, p, to, src):
        if p < chunks:
            a, b, rows = ys_main.at[p], qr_main.at[s, p], g_main
        else:
            a, b, rows = ys_tail, qr_tail.at[s], 16
        return pltpu.make_async_remote_copy(
            src_ref=a.at[pl.ds(pl.multiple_of(to * rows, 16), rows)],
            dst_ref=b.at[src],
            send_sem=z_ssem.at[p, to],
            recv_sem=z_rsem.at[s, p, src],
            device_id=(to * inner + lo, t),
            device_id_type=MESH,
        )

    def n_copy(s, to, src):
        return pltpu.make_async_remote_copy(
            src_ref=ss_send.at[pl.ds(pl.multiple_of(to * hs, 8), hs)],
            dst_ref=ss_recv.at[s, pl.ds(pl.multiple_of(src * hs, 8), hs)],
            send_sem=n_ssem.at[to],
            recv_sem=n_rsem.at[s, src],
            device_id=(to, t),
            device_id_type=MESH,
        )

    def tp_copy(s, to, src):
        return pltpu.make_async_remote_copy(
            src_ref=mix_s.at[pl.ds(pl.multiple_of(to * 8, 8), 8)],
            dst_ref=tp_recv.at[s, pl.ds(pl.multiple_of(src * 8, 8), 8)],
            send_sem=tp_ssem.at[to],
            recv_sem=tp_rsem.at[s, src],
            device_id=(r, to),
            device_id_type=MESH,
        )

    def step(s, carry):
        s8 = pl.multiple_of(s * 8, 8)
        x = state_s[...] + emb_s[pl.ds(s8, 8), :] + ctx_s[...]
        a = rms_scale(x, gl_ref[...]).astype(BF16)

        @pl.when(s == 0)
        def _():
            loads[1].wait()
            loads[2].wait()

        f = dot(a, w_in[...])
        f = (f / (1.0 + jnp.exp(-f))).astype(BF16)
        state = x + dot(f, w_out[...])
        state_s[...] = state
        slots = dot(pick_ref[s].astype(BF16), state.astype(BF16))
        for k in range(4):
            w = dl // 4
            packm[4 * k : 4 * k + 4, :] = slots[0:4, w * k : w * k + w]
        for k in range(8):
            w = dl // 8
            packt[k : k + 1, :] = slots[4:5, w * k : w * k + w]
        packed = jnp.concatenate([packm[...], packt[...]], axis=1).astype(BF16)
        ag_send[...] = packed

        def send(i, c):
            ag_rows(s, lax.rem(r + i, n_rows), r).start()
            return c

        def send_own(i, c):
            ag_own(s, lax.rem(t + i, n_tp), t).start()
            return c

        lax.fori_loop(1, n_rows, send, 0)
        lax.fori_loop(1, n_tp, send_own, 0)
        ag_recv[s, pl.ds(pl.multiple_of(me * 16, 16), 16), :] = packed

        def forward(i, c):
            row = lax.rem(r + n_rows - i, n_rows)
            ag_rows(s, r, row).wait_recv()
            for k in range(1, n_tp):
                ag_forward(s, row, lax.rem(t + k, n_tp), t).start()
            return c

        lax.fori_loop(1, n_rows, forward, 0)

        @pl.when(s == 0)
        def _():
            loads[3].wait()
            loads[4].wait()

        final = rms_scale(state, og_ref[...]).astype(BF16)
        logits_ref[:, pl.ds(pl.multiple_of(s * vocab, vocab), vocab)] = dot(final, w_vocab[...])

        def recv(i, c):
            src = lax.rem(t + n_tp - i, n_tp)

            def recv_row(row, c):
                ag_forward(s, row, t, src).wait_recv()
                return c

            return lax.fori_loop(0, n_rows, recv_row, c)

        lax.fori_loop(1, n_tp, recv, 0)

        for g in range(n_dev // 16):
            got = ag_recv[s, g * 256 : g * 256 + 256, :]
            m = dot(unpack_ref[0:256, :], got[:, 0:256]).astype(BF16)
            tl = dot(unpack_ref[256:384, :], got[:, 256:384]).astype(BF16)
            for k in range(4):
                h_s[g * 64 : g * 64 + 64, 256 * k : 256 * k + 256] = m[k * 64 : k * 64 + 64]
            for k in range(8):
                h_s[n_main + g * 16 : n_main + g * 16 + 16, 128 * k : 128 * k + 128] = tl[
                    k * 16 : k * 16 + 16
                ]
        up = dot(h_s[...], w_up[...])
        ss = jnp.broadcast_to(jnp.sum(up * up, axis=1, keepdims=True), (up.shape[0], 128))
        for g in range(n_rows):
            ss_send[g * hs : g * hs + g_main, :] = ss[g * g_main : (g + 1) * g_main]
            ss_send[g * hs + g_main : g * hs + g_main + g_tail, :] = ss[
                n_main + g * g_tail : n_main + (g + 1) * g_tail
            ]
        normed = (up * gg_ref[...].astype(F32)).astype(BF16)

        @pl.when(s == 0)
        def _():
            loads[5].wait()
            loads[6].wait()
            loads[7].wait()

        def nsend(i, c):
            n_copy(s, lax.rem(r + i, n_rows), r).start()
            return c

        lax.fori_loop(1, n_rows, nsend, 0)
        at = pl.ds(pl.multiple_of(r * hs, 8), hs)
        ss_recv[s, at, :] = ss_send[at, :]

        for p in range(chunks):
            parts = []
            for w_ref, first, width in (
                (w_q, 0, q_cols), (w_k, q_cols, kv_cols), (w_v, q_cols + kv_cols, kv_cols)
            ):
                a_col = max(p * cw, first) - first
                b_col = min((p + 1) * cw, first + width) - first
                if a_col < b_col:
                    parts.append(dot(normed, w_ref[:, a_col:b_col]))
            part = parts[0] if len(parts) == 1 else jnp.concatenate(parts, axis=1)
            for g in range(n_rows):
                pos = (g % inner) * outer + g // inner
                qs_main[p, pos * g_main : (pos + 1) * g_main, :] = part[
                    g * g_main : (g + 1) * g_main
                ].astype(BF16)
                at = pos * 16 + p * n_tp
                tail_f[at : at + n_tp, :] = part[n_main + g * n_tp : n_main + (g + 1) * n_tp]
            if p == chunks - 1:
                qs_tail[...] = tail_f[...].astype(BF16)
            for q in (p,) if p < chunks - 1 else (p, chunks):
                for i in range(1, inner):
                    x_copy(s, q, lax.rem(lo + i, inner), lo).start()

        for p in range(chunks + 1):
            for i in range(1, inner):
                x_copy(s, p, lo, lax.rem(lo + inner - i, inner)).wait_recv()
            rows = outer * (g_main if p < chunks else 16)
            mine = pl.ds(pl.multiple_of(lo * rows, 16), rows)
            y = (qs_main[p, mine, :] if p < chunks else qs_tail[mine, :]).astype(F32)
            for i in range(1, inner):
                other = lax.rem(lo + i, inner)
                y = y + (xr_main[s, p, other] if p < chunks else xr_tail[s, other]).astype(F32)
            if p < chunks:
                ys_main[p] = y.astype(BF16)
            else:
                ys_tail[...] = y.astype(BF16)
            for i in range(1, outer):
                z_copy(s, p, lax.rem(hi + i, outer), hi).start()
            if p < chunks:
                qr_main[s, p, hi] = ys_main[p, pl.ds(pl.multiple_of(hi * g_main, 16), g_main), :]
            else:
                qr_tail[s, hi] = ys_tail[pl.ds(pl.multiple_of(hi * 16, 16), 16), :]
        for i in range(1, n_rows):
            n_copy(s, r, lax.rem(r + n_rows - i, n_rows)).wait_recv()
        for p in range(chunks + 1):
            for i in range(1, outer):
                z_copy(s, p, hi, lax.rem(hi + outer - i, outer)).wait_recv()

        inv = ss_recv[s, 0:hs, :]
        tsum_v = qr_tail[s, 0].astype(F32)
        for g in range(1, outer):
            tsum_v = tsum_v + qr_tail[s, g].astype(F32)
        for g in range(1, n_rows):
            inv = inv + ss_recv[s, g * hs : (g + 1) * hs, :]
        inv = lax.rsqrt(inv * (1.0 / dg) + EPS)
        tsum[...] = tsum_v
        for h in range(cols // HD):
            k, off = (h * HD) // cw, (h * HD) % cw
            v = qr_main[s, k, 0, :, off : off + HD].astype(F32)
            for g in range(1, outer):
                v = v + qr_main[s, k, g, :, off : off + HD].astype(F32)
            qf[h * hs : h * hs + g_main, :] = (v * inv[0:g_main]).astype(BF16).astype(F32)
            tv = tsum[k * n_tp : (k + 1) * n_tp, off : off + HD]
            qf[h * hs + g_main : h * hs + g_main + g_tail, :] = (
                (tv * inv[g_main : g_main + g_tail]).astype(BF16).astype(F32)
            )

        @pl.when(s == 0)
        def _():
            loads[8].wait()
            loads[9].wait()
            loads[10].wait()

        positions = lax.broadcasted_iota(jnp.int32, (group, kc.shape[1]), 1)
        n_slots = n_tp * CAP
        pairs = []
        for tt in range(n_tp):
            for c in range(CAP):
                j = tt * 4 + c if c < 4 else g_main + tt
                for v in range(kv_local):
                    pairs.append((tt, c, j, v))
        for p, (tt, c, j, v) in enumerate(pairs):
            row = idx_ref[s * n_slots + tt * CAP + c]
            length = len_ref[s * n_slots + tt * CAP + c]
            q8 = qf[pl.ds(v * group * hs + j, group, stride=hs), :]
            nk = qf[pl.ds((n_heads + v) * hs + j, 1), :]
            keys = kc[row, :, v * HD : (v + 1) * HD]
            sc = lax.dot_general(
                q8.astype(BF16), keys, (((1,), (1,)), ((), ())), preferred_element_type=F32
            )
            scores[p * group : (p + 1) * group, :] = jnp.where(
                positions < length, sc * scale, -jnp.inf
            )
            selfs[p * group : (p + 1) * group, :] = jnp.broadcast_to(
                jnp.sum(q8 * nk, axis=1, keepdims=True) * scale, (group, 128)
            )
        sc = scores[...]
        own = selfs[:, 0:1]
        top = jnp.maximum(jnp.max(sc, axis=1, keepdims=True), own)
        w = jnp.exp(sc - top)
        wo = jnp.exp(own - top)
        inv_total = 1.0 / (jnp.sum(w, axis=1, keepdims=True) + wo)
        probs[...] = (w * inv_total).astype(BF16).astype(F32)
        owns[...] = jnp.broadcast_to((wo * inv_total).astype(BF16).astype(F32), owns.shape)
        os = n_tp * 8
        for p, (tt, c, j, v) in enumerate(pairs):
            row = idx_ref[s * n_slots + tt * CAP + c]
            nv = qf[pl.ds((n_heads + kv_local + v) * hs + j, 1), :]
            values = vc[row, :, v * HD : (v + 1) * HD]
            pr = probs[p * group : (p + 1) * group, :].astype(BF16)
            o = dot(pr, values) + owns[p * group : (p + 1) * group, :] * nv
            of[pl.ds(v * group * os + tt * 8 + c, group, stride=os), :] = o

        att = jnp.concatenate(
            [of[h * os : (h + 1) * os, :].astype(BF16) for h in range(n_heads)], axis=1
        )
        mix_s[...] = dot(att, w_mix[...])

        def tsend(i, c):
            tp_copy(s, lax.rem(t + i, n_tp), t).start()
            return c

        lax.fori_loop(1, n_tp, tsend, 0)
        at = pl.ds(pl.multiple_of(t * 8, 8), 8)
        tp_recv[s, at, :] = mix_s[at, :]

        def trecv(i, c):
            tp_copy(s, t, lax.rem(t + n_tp - i, n_tp)).wait_recv()
            return c

        lax.fori_loop(1, n_tp, trecv, 0)
        patch = tp_recv[s, 0:8, :]
        for g in range(1, n_tp):
            patch = patch + tp_recv[s, g * 8 : (g + 1) * 8, :]
        back = pickt_ref[s]
        delivered = dot(back.astype(BF16), patch.astype(BF16))
        done = jnp.sum(back, axis=1, keepdims=True) > 0.0
        ctx_s[...] = jnp.where(done, delivered, ctx_s[...])

        def drain_rows(i, c):
            to = lax.rem(r + i, n_rows)
            ag_rows(s, to, r).wait_send()
            n_copy(s, to, r).wait_send()
            return c

        def drain_own(i, c):
            ag_own(s, lax.rem(t + i, n_tp), t).wait_send()
            return c

        def drain_forward(i, c):
            for k in range(1, n_tp):
                ag_forward(s, lax.rem(r + n_rows - i, n_rows), lax.rem(t + k, n_tp), t).wait_send()
            return c

        def drain_tp(i, c):
            tp_copy(s, lax.rem(t + i, n_tp), t).wait_send()
            return c

        lax.fori_loop(1, n_rows, drain_rows, 0)
        lax.fori_loop(1, n_tp, drain_own, 0)
        lax.fori_loop(1, n_rows, drain_forward, 0)
        for p in range(chunks + 1):
            for i in range(1, inner):
                x_copy(s, p, lax.rem(lo + i, inner), lo).wait_send()
            for i in range(1, outer):
                z_copy(s, p, lax.rem(hi + i, outer), hi).wait_send()
        lax.fori_loop(1, n_tp, drain_tp, 0)
        return carry

    lax.fori_loop(0, n_steps, step, 0)
    ctx_out_ref[...] = ctx_s[...].astype(BF16)


def on_device(
    hidden, context, byte_input_codes, finish, cache_len, embed, gain_local, w_in, w_out,
    output_norm_gain, w_vocab, w_up, gain_global, w_query, w_key, w_value, key_cache,
    value_cache, w_mix,
):
    n_rows, n_tp = lax.axis_size("rows"), lax.axis_size("tp")
    t = lax.axis_index("tp")
    rows, dl = hidden.shape
    n_steps = byte_input_codes.shape[1]
    vocab = embed.shape[0]
    n_dev = n_rows * n_tp
    slots = n_tp * CAP
    q_cols, kv_cols = w_query.shape[1], w_key.shape[1]
    cols = q_cols + 2 * kv_cols
    hs = -(-slots // 8) * 8
    cache = key_cache.shape[1]
    outer = min(4, n_rows)
    inner = n_rows // outer
    chunks = 16 // n_tp
    n_heads = q_cols // HD
    att_rows = slots * n_heads
    cw = cols * n_tp // 16

    oh = (
        byte_input_codes.T.reshape(n_steps * rows, 1) == jnp.arange(vocab, dtype=jnp.int32)[None, :]
    ).astype(BF16)
    picker = slot_picker(finish.T.reshape(n_steps, n_tp, rows))
    local = jnp.sum(picker * jnp.arange(rows, dtype=jnp.int32), axis=-1)
    row_index = (local + jnp.arange(n_tp, dtype=jnp.int32)[:, None] * rows).reshape(-1)
    lengths = jnp.take(cache_len, row_index, axis=0)
    mine = lax.dynamic_index_in_dim(picker, t, 1, keepdims=False).astype(F32)
    pick = jnp.pad(mine, ((0, 0), (0, 8 - CAP), (0, 0)))
    pickt = pick.transpose(0, 2, 1)

    vm = pl.BlockSpec(memory_space=pltpu.VMEM)
    sm = pl.BlockSpec(memory_space=pltpu.SMEM)
    anys = pl.BlockSpec(memory_space=pl.ANY)
    weights = (
        embed, w_in, w_out, w_vocab, w_up, w_query, w_key, w_value, key_cache, value_cache, w_mix
    )
    dma = pltpu.SemaphoreType.DMA
    logits, ctx = pl.pallas_call(
        functools.partial(kernel, n_rows, n_tp, n_steps),
        out_shape=(
            jax.ShapeDtypeStruct((rows, n_steps * vocab), F32),
            jax.ShapeDtypeStruct((rows, dl), BF16),
        ),
        in_specs=[sm, sm] + [vm] * 9 + [anys] * len(weights),
        out_specs=(vm, vm),
        scratch_shapes=[pltpu.VMEM(w.shape, w.dtype) for w in weights]
        + [
            pltpu.VMEM((n_steps * rows, dl), F32),
            pltpu.VMEM((rows, dl), F32),
            pltpu.VMEM((rows, dl), F32),
            pltpu.VMEM((16, dl // 4), F32),
            pltpu.VMEM((16, dl // 8), F32),
            pltpu.VMEM((16, 3 * dl // 8), BF16),
            pltpu.VMEM((n_steps, n_dev * 16, 3 * dl // 8), BF16),
            pltpu.VMEM((5 * n_dev, dl), BF16),
            pltpu.VMEM((chunks, 4 * n_dev, cw), BF16),
            pltpu.VMEM((16 * n_rows, cw), F32),
            pltpu.VMEM((16 * n_rows, cw), BF16),
            pltpu.VMEM((n_steps, chunks, inner, outer * 4 * n_tp, cw), BF16),
            pltpu.VMEM((n_steps, inner, outer * 16, cw), BF16),
            pltpu.VMEM((chunks, outer * 4 * n_tp, cw), BF16),
            pltpu.VMEM((outer * 16, cw), BF16),
            pltpu.VMEM((n_steps, chunks, outer, 4 * n_tp, cw), BF16),
            pltpu.VMEM((n_steps, outer, 16, cw), BF16),
            pltpu.VMEM((n_rows * hs, 128), F32),
            pltpu.VMEM((n_steps, n_rows * hs, 128), F32),
            pltpu.VMEM((cols // HD * hs, HD), F32),
            pltpu.VMEM((16, cw), F32),
            pltpu.VMEM((att_rows, cache), F32),
            pltpu.VMEM((att_rows, 128), F32),
            pltpu.VMEM((att_rows, cache), F32),
            pltpu.VMEM((att_rows, 128), F32),
            pltpu.VMEM((n_heads * n_tp * 8, HD), F32),
            pltpu.VMEM((n_tp * 8, dl), F32),
            pltpu.VMEM((n_steps, n_tp * 8, dl), F32),
            dma((len(weights),)),
            dma((n_rows,)),
            dma((n_rows, n_tp)),
            dma((n_steps, n_dev)),
            dma((chunks + 1, inner)),
            dma((n_steps, chunks + 1, inner)),
            dma((chunks + 1, outer)),
            dma((n_steps, chunks + 1, outer)),
            dma((n_rows,)),
            dma((n_steps, n_rows)),
            dma((n_tp,)),
            dma((n_steps, n_tp)),
        ],
        compiler_params=pltpu.CompilerParams(
            collective_id=0, has_side_effects=True, vmem_limit_bytes=56 * 1024 * 1024
        ),
    )(
        row_index, lengths, hidden, context, oh, pick, pickt,
        jnp.asarray(unpack_matrix(), BF16),
        gain_local.reshape(1, -1), output_norm_gain.reshape(1, -1), gain_global.reshape(1, -1),
        *weights,
    )
    return logits.reshape(rows, n_steps, vocab), ctx


def solution(mesh):
    in_specs = (
        P(("rows", "tp"), None),
        P(("rows", "tp"), None),
        P(("rows", "tp"), None),
        P("rows", None),
        P("rows"),
        P(),
        P(),
        P(),
        P(),
        P(),
        P(),
        P(None, "rows"),
        P("rows"),
        P("rows", "tp"),
        P("rows", "tp"),
        P("rows", "tp"),
        P("rows", None, "tp"),
        P("rows", None, "tp"),
        P("tp", None),
    )
    out_specs = (P(("rows", "tp"), None, None), P(("rows", "tp"), None))
    return jax.shard_map(
        on_device, mesh=mesh, in_specs=in_specs, out_specs=out_specs, check_vma=False
    )
```

```python
import functools

import jax
import jax.numpy as jnp
import numpy as np
from jax import lax
from jax.experimental import pallas as pl
from jax.experimental.pallas import tpu as pltpu
from jax.sharding import PartitionSpec as P

HD = 128
CAP = 5
R_DEV = 8
EPS = 1e-05
MESH = pl.DeviceIdType.MESH
F32 = jnp.float32
BF16 = jnp.bfloat16


def rms_scale(values, gain):
    mean_sq = jnp.mean(values * values, axis=-1, keepdims=True)
    return values * lax.rsqrt(mean_sq + EPS) * gain


def slot_picker(finished):
    place = jnp.arange(finished.shape[-1], dtype=jnp.int32)
    before = (place[:, None] > place[None, :]).astype(jnp.int32)
    ranked = jnp.sum(finished[..., None, :] * before, axis=-1)
    slot_ids = jnp.arange(CAP, dtype=jnp.int32)
    chosen = (finished[..., None, :] == 1) & (ranked[..., None, :] == slot_ids[:, None])
    return chosen.astype(jnp.int32)


def unpack_matrix():
    m = np.zeros((384, 256), np.float32)
    for d in range(16):
        for k in range(4):
            for c in range(4):
                m[k * 64 + d * 4 + c, d * 16 + 4 * k + c] = 1
        for k in range(8):
            m[256 + k * 16 + d, d * 16 + k] = 1
    return m


def dot(a, b):
    return jnp.dot(a, b, preferred_element_type=F32)


def kernel(
    n_rows, n_tp, n_steps,
    idx_ref, len_ref, hidden_ref, context_ref, oh_ref, pick_ref, unpack_ref,
    gl_ref, og_ref, gg_ref,
    embed_hbm, w_in_hbm, w_out_hbm, w_vocab_hbm, w_up_hbm, w_q_hbm, w_k_hbm, w_v_hbm,
    kc_hbm, vc_hbm, w_mix_hbm,
    logits_ref, ctx_out_ref,
    embed, w_in, w_out, w_vocab, w_up, w_q, w_k, w_v, kc, vc, w_mix,
    emb_s, state_s, ctx_s, packm, packt, ag_send, ag_recv, h_s,
    qs_main, tail_f, qs_tail, xr_main, xr_tail, ys_main, ys_tail, qr_main, qr_tail, ss_send, ss_recv,
    qf, tsum, scores, selfs, probs, owns, of, mix_s, tp_recv,
    load_sem, ag_ssem, fw_ssem, ag_rsem, x_ssem, x_rsem, z_ssem, z_rsem, n_ssem, n_rsem,
    tp_ssem, tp_rsem,
):
    r = lax.axis_index("rows")
    t = lax.axis_index("tp")
    n_dev = n_rows * n_tp
    me = r * n_tp + t
    dl = hidden_ref.shape[1]
    q_cols, kv_cols = w_q.shape[1], w_k.shape[1]
    cols = q_cols + 2 * kv_cols
    kv_local = kv_cols // HD
    n_heads = q_cols // HD
    group = n_heads // kv_local
    n_main, n_tail = 4 * n_dev, n_dev
    g_main, g_tail = 4 * n_tp, n_tp
    chunks = 16 // n_tp
    cw = cols // chunks
    hs = -(-(CAP * n_tp) // 8) * 8
    outer = min(4, n_rows)
    inner = n_rows // outer
    hi, lo = r // inner, lax.rem(r, inner)
    vocab = w_vocab.shape[1]
    dg = n_rows * w_up.shape[1]
    scale = 1.0 / np.float32(np.sqrt(np.float32(HD)))

    loads = [
        pltpu.make_async_copy(a, b, load_sem.at[i])
        for i, (a, b) in enumerate(
            [
                (embed_hbm, embed), (w_in_hbm, w_in), (w_out_hbm, w_out),
                (w_vocab_hbm, w_vocab), (w_up_hbm, w_up), (w_q_hbm, w_q),
                (w_k_hbm, w_k), (w_v_hbm, w_v), (kc_hbm, kc), (vc_hbm, vc),
                (w_mix_hbm, w_mix),
            ]
        )
    ]
    for c in loads[:5]:
        c.start()

    barrier = pltpu.get_barrier_semaphore()

    def greet(i, carry):
        to = lax.rem(me + i, n_dev)
        pl.semaphore_signal(
            barrier, inc=1, device_id=(to // n_tp, lax.rem(to, n_tp)), device_id_type=MESH
        )
        return carry

    lax.fori_loop(1, n_dev, greet, 0)

    state_s[...] = hidden_ref[...].astype(F32)
    ctx_s[...] = context_ref[...].astype(F32)
    ss_send[...] = jnp.zeros_like(ss_send)
    of[...] = jnp.zeros_like(of)
    packt[...] = jnp.zeros_like(packt)
    loads[0].wait()
    emb_s[...] = dot(oh_ref[...], embed[...])
    pl.semaphore_wait(barrier, n_dev - 1)

    def ag_rows(s, to, src):
        slot = src * n_tp + t
        return pltpu.make_async_remote_copy(
            src_ref=ag_send,
            dst_ref=ag_recv.at[s, pl.ds(pl.multiple_of(slot * 16, 16), 16)],
            send_sem=ag_ssem.at[to],
            recv_sem=ag_rsem.at[s, slot],
            device_id=(to, t),
            device_id_type=MESH,
        )

    def ag_own(s, to, src):
        slot = r * n_tp + src
        return pltpu.make_async_remote_copy(
            src_ref=ag_send,
            dst_ref=ag_recv.at[s, pl.ds(pl.multiple_of(slot * 16, 16), 16)],
            send_sem=fw_ssem.at[r, to],
            recv_sem=ag_rsem.at[s, slot],
            device_id=(r, to),
            device_id_type=MESH,
        )

    def ag_forward(s, row, to, src):
        slot = row * n_tp + src
        at = pl.ds(pl.multiple_of(slot * 16, 16), 16)
        return pltpu.make_async_remote_copy(
            src_ref=ag_recv.at[s, at],
            dst_ref=ag_recv.at[s, at],
            send_sem=fw_ssem.at[row, to],
            recv_sem=ag_rsem.at[s, slot],
            device_id=(r, to),
            device_id_type=MESH,
        )

    def x_copy(s, p, to, src):
        if p < chunks:
            a, b, rows = qs_main.at[p], xr_main.at[s, p], outer * g_main
        else:
            a, b, rows = qs_tail, xr_tail.at[s], outer * 16
        return pltpu.make_async_remote_copy(
            src_ref=a.at[pl.ds(pl.multiple_of(to * rows, 16), rows)],
            dst_ref=b.at[src],
            send_sem=x_ssem.at[p, to],
            recv_sem=x_rsem.at[s, p, src],
            device_id=(hi * inner + to, t),
            device_id_type=MESH,
        )

    def z_copy(s, p, to, src):
        if p < chunks:
            a, b, rows = ys_main.at[p], qr_main.at[s, p], g_main
        else:
            a, b, rows = ys_tail, qr_tail.at[s], 16
        return pltpu.make_async_remote_copy(
            src_ref=a.at[pl.ds(pl.multiple_of(to * rows, 16), rows)],
            dst_ref=b.at[src],
            send_sem=z_ssem.at[p, to],
            recv_sem=z_rsem.at[s, p, src],
            device_id=(to * inner + lo, t),
            device_id_type=MESH,
        )

    def n_copy(s, to, src):
        return pltpu.make_async_remote_copy(
            src_ref=ss_send.at[pl.ds(pl.multiple_of(to * hs, 8), hs)],
            dst_ref=ss_recv.at[s, pl.ds(pl.multiple_of(src * hs, 8), hs)],
            send_sem=n_ssem.at[to],
            recv_sem=n_rsem.at[s, src],
            device_id=(to, t),
            device_id_type=MESH,
        )

    def tp_copy(s, to, src):
        return pltpu.make_async_remote_copy(
            src_ref=mix_s.at[pl.ds(pl.multiple_of(to * 8, 8), 8)],
            dst_ref=tp_recv.at[s, pl.ds(pl.multiple_of(src * 8, 8), 8)],
            send_sem=tp_ssem.at[to],
            recv_sem=tp_rsem.at[s, src],
            device_id=(r, to),
            device_id_type=MESH,
        )

    def step(s, carry):
        s8 = pl.multiple_of(s * 8, 8)
        x = state_s[...] + emb_s[pl.ds(s8, 8), :] + ctx_s[...]
        a = rms_scale(x, gl_ref[...]).astype(BF16)

        @pl.when(s == 0)
        def _():
            loads[1].wait()
            loads[2].wait()
            for c in loads[5:]:
                c.start()

        f = dot(a, w_in[...])
        f = (f / (1.0 + jnp.exp(-f))).astype(BF16)
        state = x + dot(f, w_out[...])
        state_s[...] = state
        slots = dot(pick_ref[s].astype(BF16), state.astype(BF16))
        for k in range(4):
            w = dl // 4
            packm[4 * k : 4 * k + 4, :] = slots[0:4, w * k : w * k + w]
        for k in range(8):
            w = dl // 8
            packt[k : k + 1, :] = slots[4:5, w * k : w * k + w]
        packed = jnp.concatenate([packm[...], packt[...]], axis=1).astype(BF16)
        ag_send[...] = packed

        def send(i, c):
            ag_rows(s, lax.rem(r + i, n_rows), r).start()
            return c

        def send_own(i, c):
            ag_own(s, lax.rem(t + i, n_tp), t).start()
            return c

        lax.fori_loop(1, n_rows, send, 0)
        lax.fori_loop(1, n_tp, send_own, 0)
        ag_recv[s, pl.ds(pl.multiple_of(me * 16, 16), 16), :] = packed

        def forward(i, c):
            row = lax.rem(r + n_rows - i, n_rows)
            ag_rows(s, r, row).wait_recv()
            for k in range(1, n_tp):
                ag_forward(s, row, lax.rem(t + k, n_tp), t).start()
            return c

        lax.fori_loop(1, n_rows, forward, 0)

        @pl.when(s == 0)
        def _():
            loads[3].wait()
            loads[4].wait()

        final = rms_scale(state, og_ref[...]).astype(BF16)
        logits_ref[:, pl.ds(pl.multiple_of(s * vocab, vocab), vocab)] = dot(final, w_vocab[...])

        def recv(i, c):
            src = lax.rem(t + n_tp - i, n_tp)

            def recv_row(row, c):
                ag_forward(s, row, t, src).wait_recv()
                return c

            return lax.fori_loop(0, n_rows, recv_row, c)

        lax.fori_loop(1, n_tp, recv, 0)

        for g in range(n_dev // 16):
            got = ag_recv[s, g * 256 : g * 256 + 256, :]
            m = dot(unpack_ref[0:256, :], got[:, 0:256]).astype(BF16)
            tl = dot(unpack_ref[256:384, :], got[:, 256:384]).astype(BF16)
            for k in range(4):
                h_s[g * 64 : g * 64 + 64, 256 * k : 256 * k + 256] = m[k * 64 : k * 64 + 64]
            for k in range(8):
                h_s[n_main + g * 16 : n_main + g * 16 + 16, 128 * k : 128 * k + 128] = tl[
                    k * 16 : k * 16 + 16
                ]
        up = dot(h_s[...], w_up[...])
        ss = jnp.broadcast_to(jnp.sum(up * up, axis=1, keepdims=True), (up.shape[0], 128))
        for g in range(n_rows):
            ss_send[g * hs : g * hs + g_main, :] = ss[g * g_main : (g + 1) * g_main]
            ss_send[g * hs + g_main : g * hs + g_main + g_tail, :] = ss[
                n_main + g * g_tail : n_main + (g + 1) * g_tail
            ]
        normed = (up * gg_ref[...].astype(F32)).astype(BF16)

        @pl.when(s == 0)
        def _():
            loads[5].wait()
            loads[6].wait()
            loads[7].wait()

        def nsend(i, c):
            n_copy(s, lax.rem(r + i, n_rows), r).start()
            return c

        lax.fori_loop(1, n_rows, nsend, 0)
        at = pl.ds(pl.multiple_of(r * hs, 8), hs)
        ss_recv[s, at, :] = ss_send[at, :]

        for p in range(chunks):
            parts = []
            for w_ref, first, width in (
                (w_q, 0, q_cols), (w_k, q_cols, kv_cols), (w_v, q_cols + kv_cols, kv_cols)
            ):
                a_col = max(p * cw, first) - first
                b_col = min((p + 1) * cw, first + width) - first
                if a_col < b_col:
                    parts.append(dot(normed, w_ref[:, a_col:b_col]))
            part = parts[0] if len(parts) == 1 else jnp.concatenate(parts, axis=1)
            for g in range(n_rows):
                pos = (g % inner) * outer + g // inner
                qs_main[p, pos * g_main : (pos + 1) * g_main, :] = part[
                    g * g_main : (g + 1) * g_main
                ].astype(BF16)
                at = pos * 16 + p * n_tp
                tail_f[at : at + n_tp, :] = part[n_main + g * n_tp : n_main + (g + 1) * n_tp]
            if p == chunks - 1:
                qs_tail[...] = tail_f[...].astype(BF16)
            for q in (p,) if p < chunks - 1 else (p, chunks):
                for i in range(1, inner):
                    x_copy(s, q, lax.rem(lo + i, inner), lo).start()

        for p in range(chunks + 1):
            for i in range(1, inner):
                x_copy(s, p, lo, lax.rem(lo + inner - i, inner)).wait_recv()
            rows = outer * (g_main if p < chunks else 16)
            mine = pl.ds(pl.multiple_of(lo * rows, 16), rows)
            y = (qs_main[p, mine, :] if p < chunks else qs_tail[mine, :]).astype(F32)
            for i in range(1, inner):
                other = lax.rem(lo + i, inner)
                y = y + (xr_main[s, p, other] if p < chunks else xr_tail[s, other]).astype(F32)
            if p < chunks:
                ys_main[p] = y.astype(BF16)
            else:
                ys_tail[...] = y.astype(BF16)
            for i in range(1, outer):
                z_copy(s, p, lax.rem(hi + i, outer), hi).start()
            if p < chunks:
                qr_main[s, p, hi] = ys_main[p, pl.ds(pl.multiple_of(hi * g_main, 16), g_main), :]
            else:
                qr_tail[s, hi] = ys_tail[pl.ds(pl.multiple_of(hi * 16, 16), 16), :]
        for i in range(1, n_rows):
            n_copy(s, r, lax.rem(r + n_rows - i, n_rows)).wait_recv()
        for p in range(chunks + 1):
            for i in range(1, outer):
                z_copy(s, p, hi, lax.rem(hi + outer - i, outer)).wait_recv()

        inv = ss_recv[s, 0:hs, :]
        tsum_v = qr_tail[s, 0].astype(F32)
        for g in range(1, outer):
            tsum_v = tsum_v + qr_tail[s, g].astype(F32)
        for g in range(1, n_rows):
            inv = inv + ss_recv[s, g * hs : (g + 1) * hs, :]
        inv = lax.rsqrt(inv * (1.0 / dg) + EPS)
        tsum[...] = tsum_v
        for h in range(cols // HD):
            k, off = (h * HD) // cw, (h * HD) % cw
            v = qr_main[s, k, 0, :, off : off + HD].astype(F32)
            for g in range(1, outer):
                v = v + qr_main[s, k, g, :, off : off + HD].astype(F32)
            qf[h * hs : h * hs + g_main, :] = (v * inv[0:g_main]).astype(BF16).astype(F32)
            tv = tsum[k * n_tp : (k + 1) * n_tp, off : off + HD]
            qf[h * hs + g_main : h * hs + g_main + g_tail, :] = (
                (tv * inv[g_main : g_main + g_tail]).astype(BF16).astype(F32)
            )

        @pl.when(s == 0)
        def _():
            loads[8].wait()
            loads[9].wait()
            loads[10].wait()

        positions = lax.broadcasted_iota(jnp.int32, (group, kc.shape[1]), 1)
        n_slots = n_tp * CAP
        pairs = []
        for tt in range(n_tp):
            for c in range(CAP):
                j = tt * 4 + c if c < 4 else g_main + tt
                for v in range(kv_local):
                    pairs.append((tt, c, j, v))
        for p, (tt, c, j, v) in enumerate(pairs):
            row = idx_ref[s * n_slots + tt * CAP + c]
            length = len_ref[row]
            q8 = qf[pl.ds(v * group * hs + j, group, stride=hs), :]
            nk = qf[pl.ds((n_heads + v) * hs + j, 1), :]
            keys = kc[row, :, v * HD : (v + 1) * HD]
            sc = lax.dot_general(
                q8.astype(BF16), keys, (((1,), (1,)), ((), ())), preferred_element_type=F32
            )
            scores[p * group : (p + 1) * group, :] = jnp.where(
                positions < length, sc * scale, -jnp.inf
            )
            selfs[p * group : (p + 1) * group, :] = jnp.broadcast_to(
                jnp.sum(q8 * nk, axis=1, keepdims=True) * scale, (group, 128)
            )
        sc = scores[...]
        own = selfs[:, 0:1]
        top = jnp.maximum(jnp.max(sc, axis=1, keepdims=True), own)
        w = jnp.exp(sc - top)
        wo = jnp.exp(own - top)
        inv_total = 1.0 / (jnp.sum(w, axis=1, keepdims=True) + wo)
        probs[...] = (w * inv_total).astype(BF16).astype(F32)
        owns[...] = jnp.broadcast_to((wo * inv_total).astype(BF16).astype(F32), owns.shape)
        os = n_tp * 8
        for p, (tt, c, j, v) in enumerate(pairs):
            row = idx_ref[s * n_slots + tt * CAP + c]
            nv = qf[pl.ds((n_heads + kv_local + v) * hs + j, 1), :]
            values = vc[row, :, v * HD : (v + 1) * HD]
            pr = probs[p * group : (p + 1) * group, :].astype(BF16)
            o = dot(pr, values) + owns[p * group : (p + 1) * group, :] * nv
            of[pl.ds(v * group * os + tt * 8 + c, group, stride=os), :] = o

        att = jnp.concatenate(
            [of[h * os : (h + 1) * os, :].astype(BF16) for h in range(n_heads)], axis=1
        )
        mix_s[...] = dot(att, w_mix[...])

        def tsend(i, c):
            tp_copy(s, lax.rem(t + i, n_tp), t).start()
            return c

        lax.fori_loop(1, n_tp, tsend, 0)
        at = pl.ds(pl.multiple_of(t * 8, 8), 8)
        tp_recv[s, at, :] = mix_s[at, :]

        def trecv(i, c):
            tp_copy(s, t, lax.rem(t + n_tp - i, n_tp)).wait_recv()
            return c

        lax.fori_loop(1, n_tp, trecv, 0)
        patch = tp_recv[s, 0:8, :]
        for g in range(1, n_tp):
            patch = patch + tp_recv[s, g * 8 : (g + 1) * 8, :]
        back = pick_ref[s].astype(BF16)
        to_rows = (((0,), (0,)), ((), ()))
        delivered = lax.dot_general(
            back, patch.astype(BF16), to_rows, preferred_element_type=F32
        )
        done = (
            lax.dot_general(
                back, jnp.ones((8, 128), BF16), to_rows, preferred_element_type=F32
            )[:, 0:1]
            > 0.0
        )
        ctx_s[...] = jnp.where(done, delivered, ctx_s[...])

        def drain_rows(i, c):
            to = lax.rem(r + i, n_rows)
            ag_rows(s, to, r).wait_send()
            n_copy(s, to, r).wait_send()
            return c

        def drain_own(i, c):
            ag_own(s, lax.rem(t + i, n_tp), t).wait_send()
            return c

        def drain_forward(i, c):
            for k in range(1, n_tp):
                ag_forward(s, lax.rem(r + n_rows - i, n_rows), lax.rem(t + k, n_tp), t).wait_send()
            return c

        def drain_tp(i, c):
            tp_copy(s, lax.rem(t + i, n_tp), t).wait_send()
            return c

        lax.fori_loop(1, n_rows, drain_rows, 0)
        lax.fori_loop(1, n_tp, drain_own, 0)
        lax.fori_loop(1, n_rows, drain_forward, 0)
        for p in range(chunks + 1):
            for i in range(1, inner):
                x_copy(s, p, lax.rem(lo + i, inner), lo).wait_send()
            for i in range(1, outer):
                z_copy(s, p, lax.rem(hi + i, outer), hi).wait_send()
        lax.fori_loop(1, n_tp, drain_tp, 0)
        return carry

    lax.fori_loop(0, n_steps, step, 0)
    ctx_out_ref[...] = ctx_s[...].astype(BF16)


def on_device(
    hidden, context, byte_input_codes, finish, cache_len, embed, gain_local, w_in, w_out,
    output_norm_gain, w_vocab, w_up, gain_global, w_query, w_key, w_value, key_cache,
    value_cache, w_mix,
):
    n_rows, n_tp = lax.axis_size("rows"), lax.axis_size("tp")
    t = lax.axis_index("tp")
    rows, dl = hidden.shape
    n_steps = byte_input_codes.shape[1]
    vocab = embed.shape[0]
    n_dev = n_rows * n_tp
    slots = n_tp * CAP
    q_cols, kv_cols = w_query.shape[1], w_key.shape[1]
    cols = q_cols + 2 * kv_cols
    hs = -(-slots // 8) * 8
    cache = key_cache.shape[1]
    outer = min(4, n_rows)
    inner = n_rows // outer
    chunks = 16 // n_tp
    n_heads = q_cols // HD
    att_rows = slots * n_heads
    cw = cols * n_tp // 16

    oh = (
        byte_input_codes.T.reshape(n_steps * rows, 1) == jnp.arange(vocab, dtype=jnp.int32)[None, :]
    ).astype(BF16)
    picker = slot_picker(finish.T.reshape(n_steps, n_tp, rows))
    local = jnp.sum(picker * jnp.arange(rows, dtype=jnp.int32), axis=-1)
    row_index = (local + jnp.arange(n_tp, dtype=jnp.int32)[:, None] * rows).reshape(-1)
    mine = lax.dynamic_index_in_dim(picker, t, 1, keepdims=False).astype(F32)
    pick = jnp.pad(mine, ((0, 0), (0, 8 - CAP), (0, 0)))

    vm = pl.BlockSpec(memory_space=pltpu.VMEM)
    sm = pl.BlockSpec(memory_space=pltpu.SMEM)
    anys = pl.BlockSpec(memory_space=pl.ANY)
    weights = (
        embed, w_in, w_out, w_vocab, w_up, w_query, w_key, w_value, key_cache, value_cache, w_mix
    )
    dma = pltpu.SemaphoreType.DMA
    logits, ctx = pl.pallas_call(
        functools.partial(kernel, n_rows, n_tp, n_steps),
        out_shape=(
            jax.ShapeDtypeStruct((rows, n_steps * vocab), F32),
            jax.ShapeDtypeStruct((rows, dl), BF16),
        ),
        in_specs=[sm, sm] + [vm] * 8 + [anys] * len(weights),
        out_specs=(vm, vm),
        scratch_shapes=[pltpu.VMEM(w.shape, w.dtype) for w in weights]
        + [
            pltpu.VMEM((n_steps * rows, dl), F32),
            pltpu.VMEM((rows, dl), F32),
            pltpu.VMEM((rows, dl), F32),
            pltpu.VMEM((16, dl // 4), F32),
            pltpu.VMEM((16, dl // 8), F32),
            pltpu.VMEM((16, 3 * dl // 8), BF16),
            pltpu.VMEM((n_steps, n_dev * 16, 3 * dl // 8), BF16),
            pltpu.VMEM((5 * n_dev, dl), BF16),
            pltpu.VMEM((chunks, 4 * n_dev, cw), BF16),
            pltpu.VMEM((16 * n_rows, cw), F32),
            pltpu.VMEM((16 * n_rows, cw), BF16),
            pltpu.VMEM((n_steps, chunks, inner, outer * 4 * n_tp, cw), BF16),
            pltpu.VMEM((n_steps, inner, outer * 16, cw), BF16),
            pltpu.VMEM((chunks, outer * 4 * n_tp, cw), BF16),
            pltpu.VMEM((outer * 16, cw), BF16),
            pltpu.VMEM((n_steps, chunks, outer, 4 * n_tp, cw), BF16),
            pltpu.VMEM((n_steps, outer, 16, cw), BF16),
            pltpu.VMEM((n_rows * hs, 128), F32),
            pltpu.VMEM((n_steps, n_rows * hs, 128), F32),
            pltpu.VMEM((cols // HD * hs, HD), F32),
            pltpu.VMEM((16, cw), F32),
            pltpu.VMEM((att_rows, cache), F32),
            pltpu.VMEM((att_rows, 128), F32),
            pltpu.VMEM((att_rows, cache), F32),
            pltpu.VMEM((att_rows, 128), F32),
            pltpu.VMEM((n_heads * n_tp * 8, HD), F32),
            pltpu.VMEM((n_tp * 8, dl), F32),
            pltpu.VMEM((n_steps, n_tp * 8, dl), F32),
            dma((len(weights),)),
            dma((n_rows,)),
            dma((n_rows, n_tp)),
            dma((n_steps, n_dev)),
            dma((chunks + 1, inner)),
            dma((n_steps, chunks + 1, inner)),
            dma((chunks + 1, outer)),
            dma((n_steps, chunks + 1, outer)),
            dma((n_rows,)),
            dma((n_steps, n_rows)),
            dma((n_tp,)),
            dma((n_steps, n_tp)),
        ],
        compiler_params=pltpu.CompilerParams(
            collective_id=0, has_side_effects=True, vmem_limit_bytes=56 * 1024 * 1024
        ),
    )(
        row_index, cache_len, hidden, context, oh, pick,
        jnp.asarray(unpack_matrix(), BF16),
        gain_local.reshape(1, -1), output_norm_gain.reshape(1, -1), gain_global.reshape(1, -1),
        *weights,
    )
    return logits.reshape(rows, n_steps, vocab), ctx


def solution(mesh):
    in_specs = (
        P(("rows", "tp"), None),
        P(("rows", "tp"), None),
        P(("rows", "tp"), None),
        P("rows", None),
        P("rows"),
        P(),
        P(),
        P(),
        P(),
        P(),
        P(),
        P(None, "rows"),
        P("rows"),
        P("rows", "tp"),
        P("rows", "tp"),
        P("rows", "tp"),
        P("rows", None, "tp"),
        P("rows", None, "tp"),
        P("tp", None),
    )
    out_specs = (P(("rows", "tp"), None, None), P(("rows", "tp"), None))
    return jax.shard_map(
        on_device, mesh=mesh, in_specs=in_specs, out_specs=out_specs, check_vma=False
    )
```
